32 devices in a mesh: region: 4 (over x, core), dom: 8 (over z, y).
Axes of the slice: x: 2, y: 2, z: 4, core: 2. Of those that a mesh axis runs over, the one named last changes fastest.
Arguments:
- x_init: bfloat16 [131072, 128], P(('region', 'dom')), may hold values from -6 to 6
- tiles: bfloat16 [9216, 128, 128], P(('region', 'dom'))
- tile_row: int32 [9216], P(('region', 'dom')), may hold values from 0 to 31
- tile_col: int32 [9216], P(('region', 'dom')), may hold values from 0 to 63, as said below
- send_list: int32 [32, 4, 8], P(('region', 'dom')), may hold values from 0 to 31, as said below
- send_count: int32 [32, 4], P(('region', 'dom')), may hold values from 1 to 8, as said below
Outputs:
- basis: bfloat16 [131072, 128], P(('region', 'dom'))
- ritz_matrix: float32 [2, 128, 128], replicated
The draws below stay inside these ranges and needn't reach their ends.
Inputs may be any that keep to these rules, and one draw needn't show every extreme that they name: `send_list`: the 8 entries of one partition and direction are distinct row tiles of that partition. `send_count`: some partition sends 8 row tiles in every direction. `tile_col`: a value 32 + d * 8 + s with d = 0 .. 3 names slot s of the d-th received stack of extended, and s is below the count that this neighbour sends; no value names a stack where the neighbour does not exist.
All inputs are finite; a program needn't handle non-finite values.
Results may differ from the reference program's by a relative error of at most 0.00115.
The reference program's roundings to bfloat16 on the way count: a program that leaves them out, or rounds other values in their place, can miss the bound.
Values may be sent and summed in bfloat16 or wider, within the bound.
A program may use at most 64 MiB of HBM per device.

```python
import math
import jax
import jax.numpy as jnp
from jax import lax

K = 128
B = 128
RT = 32
NTD = 288
CAP = 8
ITERS = 2
REGIONS = 4
PER_REGION = 8
PARTITIONS = 32
NODES = 131072


def link_counts(key):
    seeded = jax.random.fold_in(key, 11)
    count_parts = REGIONS * PER_REGION
    counts = jax.random.randint(jax.random.fold_in(seeded, 1), (count_parts, 4), 1, CAP + 1)
    chosen = jax.random.randint(jax.random.fold_in(seeded, 2), (), 0, count_parts - 1)
    part_ids = jnp.arange(count_parts)[:, None]
    dir_ids = jnp.arange(4)[None, :]
    counts = jnp.where(part_ids == chosen, CAP, counts)
    counts = jnp.where((part_ids == PER_REGION) & (dir_ids == 3), CAP, counts)
    counts = jnp.where((part_ids == count_parts - 1) & (dir_ids == 0), 1, counts)
    return counts.astype(jnp.int32)


def draw_send_count(key, part):
    return link_counts(key)


def draw_send_list(key, part):
    count_parts = REGIONS * PER_REGION
    keys = jax.random.split(jax.random.fold_in(key, 23), count_parts * 4)
    positions = jnp.arange(RT, dtype=jnp.int32)

    def one_list(single, index):
        order = jax.random.permutation(single, RT).astype(jnp.int32)
        first = order[0]
        moved = jnp.where(order == RT - 1, first, jnp.where(positions == 0, RT - 1, order))
        second = moved[1]
        moved = jnp.where(moved == 0, second, jnp.where(positions == 1, 0, moved))
        return jnp.where(index == 0, moved, order)[:CAP]
    lists = jax.vmap(one_list)(keys, jnp.arange(count_parts * 4, dtype=jnp.int32))
    return lists.reshape(count_parts, 4, CAP).astype(jnp.int32)


def draw_tile_col(key, part):
    count_parts = REGIONS * PER_REGION
    counts = link_counts(key).reshape(REGIONS, PER_REGION, 4)
    zero_dom = jnp.zeros((REGIONS, 1), jnp.int32)
    zero_region = jnp.zeros((1, PER_REGION), jnp.int32)
    live_lower_dom = jnp.concatenate([zero_dom, counts[:, :-1, 0]], axis=1)
    live_upper_dom = jnp.concatenate([counts[:, 1:, 1], zero_dom], axis=1)
    live_lower_region = jnp.concatenate([zero_region, counts[:-1, :, 2]], axis=0)
    live_upper_region = jnp.concatenate([counts[1:, :, 3], zero_region], axis=0)
    live_counts = jnp.stack([live_lower_dom, live_upper_dom, live_lower_region, live_upper_region], axis=-1)
    live_counts = live_counts.reshape(count_parts, 4)
    seeded = jax.random.fold_in(key, 37)
    category = jax.random.randint(jax.random.fold_in(seeded, 1), (count_parts, NTD), 0, 8)
    own_tile = jax.random.randint(jax.random.fold_in(seeded, 2), (count_parts, NTD), 0, RT)
    slot_draw = jax.random.randint(jax.random.fold_in(seeded, 3), (count_parts, NTD), 0, 65520)
    direction = jnp.clip(category - 4, 0, 3)
    available = jnp.take_along_axis(live_counts, direction, axis=1)
    slot_index = slot_draw % jnp.maximum(available, 1)
    remote = RT + direction * CAP + slot_index
    use_remote = (category >= 4) & (available > 0)
    result = jnp.where(use_remote, remote, own_tile)
    part_ids = jnp.arange(count_parts)[:, None]
    tile_ids = jnp.arange(NTD)[None, :]
    result = jnp.where((part_ids == 0) & (tile_ids == 0), RT + 4 * CAP - 1, result)
    result = jnp.where((part_ids == 0) & (tile_ids == 1), 0, result)
    return result.reshape(count_parts * NTD).astype(jnp.int32)


def draw_tiles(key, part):
    count_parts = REGIONS * PER_REGION
    fan_total = B * NTD // RT
    seeded = jax.random.fold_in(key, 53)
    rising = 3.0 ** (jnp.arange(count_parts, dtype=jnp.float32) / max(count_parts - 1, 1))
    values = jax.random.normal(seeded, (count_parts, NTD, B, B), jnp.float32)
    values = values * (rising[:, None, None, None] / math.sqrt(fan_total))
    return values.reshape(count_parts * NTD, B, B).astype(jnp.bfloat16)


def plant(array, rng, least, high):
    spot = [jax.random.randint(jax.random.fold_in(rng, axis), (), 0, length) for axis, length in enumerate(array.shape)]
    main_axis = array.shape.index(max(array.shape))
    beside = spot[:main_axis] + [(spot[main_axis] + 1) % array.shape[main_axis]] + spot[main_axis + 1:]
    return array.at[tuple(spot)].set(least).at[tuple(beside)].set(high)


def block_scale(rng, dims, shards, least, high):
    gain = 1.0
    for axis_at, blocks in shards:
        steps = jax.random.uniform(jax.random.fold_in(jax.random.fold_in(rng, 6), axis_at), (blocks,), jnp.float32, least / len(shards), high / len(shards))
        gain = gain * jnp.repeat(jnp.exp(steps), dims[axis_at] // blocks).reshape((-1,) + (1,) * (len(dims) - 1 - axis_at))
    return gain


def scatter_about(rng, extent, spread, limit, cuts=(), kind=jnp.bfloat16):
    array = spread * jax.random.normal(rng, extent, jnp.float32)
    if cuts:
        array = array * block_scale(rng, extent, cuts, -0.22, 0.18)
    return jnp.clip(array, -limit, limit).astype(kind)


def setup_inputs(seed: int = 0) -> dict:
    key_list = jax.random.split(jax.random.key(seed), 7)
    x_init = scatter_about(key_list[0], (NODES, K), 1.0, 6.0, ((0, 32),))
    tiles = draw_tiles(jax.random.fold_in(key_list[6], 71), 0)
    tile_row = plant(jax.random.randint(key_list[2], (PARTITIONS * NTD,), 0, RT), jax.random.fold_in(key_list[2], 1), 0, RT - 1).astype(jnp.int32)
    tile_col = draw_tile_col(jax.random.fold_in(key_list[6], 71), 0)
    send_list = draw_send_list(jax.random.fold_in(key_list[6], 71), 0)
    send_count = draw_send_count(jax.random.fold_in(key_list[6], 71), 0)
    return dict(x_init=x_init, tiles=tiles, tile_row=tile_row, tile_col=tile_col, send_list=send_list, send_count=send_count)


def gram_of(current, node_total):
    return jnp.dot(current.T.astype(jnp.float32), current.astype(jnp.float32), preferred_element_type=jnp.float32) / node_total

def apply_graph(basis, tiles, tile_row, tile_col, send_list, send_count):
    count_parts = PARTITIONS
    blocks = basis.reshape(count_parts, RT, B, K)
    slots = jnp.arange(CAP, dtype=jnp.int32)
    live_slot = slots[None, None, :] < send_count[:, :, None]
    picked = jax.vmap(lambda own_tiles, row_list: own_tiles[row_list])(blocks, send_list)
    sends = jnp.where(live_slot[:, :, :, None, None], picked, jnp.zeros_like(picked))
    grid = sends.reshape(REGIONS, PER_REGION, 4, CAP, B, K)
    zero_dom = jnp.zeros_like(grid[:, :1, 0])
    from_lower_dom = jnp.concatenate([zero_dom, grid[:, :-1, 0]], axis=1)
    from_upper_dom = jnp.concatenate([grid[:, 1:, 1], zero_dom], axis=1)
    zero_region = jnp.zeros_like(grid[:1, :, 2])
    from_lower_region = jnp.concatenate([zero_region, grid[:-1, :, 2]], axis=0)
    from_upper_region = jnp.concatenate([grid[1:, :, 3], zero_region], axis=0)
    received = jnp.stack([from_lower_dom, from_upper_dom, from_lower_region, from_upper_region], axis=2)
    received = received.reshape(count_parts, 4 * CAP, B, K)

    def one_part(pieces):
        own_tiles, incoming, part_tiles, part_rows, part_cols = pieces
        extended = jnp.concatenate([own_tiles, incoming], axis=0)
        gathered = extended[part_cols].astype(jnp.float32)
        products = jnp.einsum('tij,tjk->tik', part_tiles.astype(jnp.float32), gathered, precision=lax.Precision.HIGHEST)
        return jax.ops.segment_sum(products, part_rows, num_segments=RT)
    applied = lax.map(one_part, (blocks, received, tiles.reshape(count_parts, NTD, B, B), tile_row.reshape(count_parts, NTD), tile_col.reshape(count_parts, NTD)))
    return applied.reshape(count_parts * RT * B, K)

def reference(x_init, tiles, tile_row, tile_col, send_list, send_count):
    node_total = x_init.shape[0]
    current = x_init
    gram = gram_of(current, node_total)
    identity = jnp.eye(K, dtype=jnp.float32)
    rayleigh_list = []
    basis = x_init
    for iteration in range(ITERS):
        factor = jnp.linalg.cholesky(gram)
        inverse = lax.linalg.triangular_solve(factor, identity, left_side=True, lower=True)
        basis = jnp.dot(current.astype(jnp.float32), inverse.T, precision=lax.Precision.HIGHEST).astype(jnp.bfloat16)
        applied = apply_graph(basis, tiles, tile_row, tile_col, send_list, send_count)
        rayleigh = jnp.dot(basis.astype(jnp.float32).T, applied, precision=lax.Precision.HIGHEST) / math.sqrt(node_total)
        rayleigh_list.append(rayleigh)
        current = applied.astype(jnp.bfloat16)
        if iteration + 1 < ITERS:
            gram = gram_of(current, node_total)
    return (basis, jnp.stack(rayleigh_list))
```

```python
import functools
import math

import jax
import jax.numpy as jnp
from jax import lax
from jax.experimental import pallas as pl
from jax.experimental.pallas import tpu as pltpu
from jax.sharding import PartitionSpec as P

ITERS = 2
F32 = jnp.float32
BF16 = jnp.bfloat16
MESH = pl.DeviceIdType.MESH
VM = pl.BlockSpec(memory_space=pltpu.VMEM)
SM = pl.BlockSpec(memory_space=pltpu.SMEM)
LIMIT = 48 * 1024 * 1024


def reduce_kernel(regions, doms, pieces, x_ref, o_ref, scat, res, send_a, recv_a, send_b, recv_b):
    total = regions * doms
    stride = total // pieces
    me = lax.axis_index("dom") * regions + lax.axis_index("region")
    mine = me // stride
    owner = lax.rem(me, stride) == 0

    def device(flat):
        return (lax.rem(flat, regions), flat // regions)

    barrier = pltpu.get_barrier_semaphore()

    def greet(off, carry):
        pl.semaphore_signal(
            barrier, inc=1, device_id=device(lax.rem(me + off, total)), device_id_type=MESH
        )
        return carry

    lax.fori_loop(1, total, greet, 0)
    pl.semaphore_wait(barrier, total - 1)

    def scatter(step, carry):
        piece = lax.rem(mine + step, pieces)
        target = piece * stride

        @pl.when(target != me)
        def _():
            pltpu.make_async_remote_copy(
                src_ref=x_ref.at[piece],
                dst_ref=scat.at[lax.rem(me - target - 1 + total, total)],
                send_sem=send_a,
                recv_sem=recv_a,
                device_id=device(target),
                device_id_type=MESH,
            ).start()

        return carry

    lax.fori_loop(0, pieces, scatter, 0)

    @pl.when(owner)
    def _():
        pltpu.make_async_copy(scat, scat, recv_a).wait()
        parts = [scat[s] for s in range(total - 1)] + [x_ref[mine]]
        while len(parts) > 1:
            parts = [a + b for a, b in zip(parts[::2], parts[1::2])] + (
                [parts[-1]] if len(parts) % 2 else []
            )
        res[mine] = parts[0]

        def spread(off, carry):
            pltpu.make_async_remote_copy(
                src_ref=res.at[mine],
                dst_ref=res.at[mine],
                send_sem=send_b,
                recv_sem=recv_b,
                device_id=device(lax.rem(me + off, total)),
                device_id_type=MESH,
            ).start()
            return carry

        lax.fori_loop(1, total, spread, 0)
        rest = res.at[pl.ds(0, pieces - 1)]
        pltpu.make_async_copy(rest, rest, recv_b).wait()
        sent = x_ref.at[pl.ds(0, pieces - 1)]
        pltpu.make_async_copy(sent, sent, send_a).wait()
        pltpu.make_async_copy(scat, scat, send_b).wait()

    @pl.when(jnp.logical_not(owner))
    def _():
        pltpu.make_async_copy(res, res, recv_b).wait()
        pltpu.make_async_copy(x_ref, x_ref, send_a).wait()

    o_ref[...] = res[...]


def all_sum(x, regions, doms, ident):
    rows, lanes = x.shape
    total = regions * doms
    pieces = min(total, 16)
    shape = (pieces, rows // pieces, lanes)
    out = pl.pallas_call(
        functools.partial(reduce_kernel, regions, doms, pieces),
        out_shape=jax.ShapeDtypeStruct(shape, F32),
        in_specs=[VM],
        out_specs=VM,
        scratch_shapes=[
            pltpu.VMEM((total - 1,) + shape[1:], F32),
            pltpu.VMEM(shape, F32),
            pltpu.SemaphoreType.DMA,
            pltpu.SemaphoreType.DMA,
            pltpu.SemaphoreType.DMA,
            pltpu.SemaphoreType.DMA,
        ],
        compiler_params=pltpu.CompilerParams(collective_id=ident, has_side_effects=True),
        name="allsum" + str(ident),
    )(x.reshape(shape))
    return out.reshape(rows, lanes)


def invert_rows(gram, out_ref):
    size = gram.shape[0]
    tiles = [gram[8 * j : 8 * j + 8, :] for j in range(size // 8)]
    lane = lax.broadcasted_iota(jnp.int32, (8, size), 1)
    sub = lax.broadcasted_iota(jnp.int32, (8, size), 0)
    lane1 = lax.broadcasted_iota(jnp.int32, (1, size), 1)
    for k in range(size):
        kb, ks = divmod(k, 8)
        row = tiles[kb][ks : ks + 1, :]
        pivot = jnp.broadcast_to(row[:, k : k + 1], (1, size))
        row = jnp.where(lane1 == k, 1.0, row)
        root = lax.rsqrt(pivot)
        root = root * (1.5 - 0.5 * pivot * root * root)
        out_ref[k : k + 1, :] = jnp.where(lane1 <= k, row * root, 0.0)
        scaled = row * (root * root)
        here = lane == k
        for j in range(kb, size // 8):
            col = jnp.broadcast_to(tiles[j][:, k : k + 1], (8, size))
            if j == kb:
                if ks == 7:
                    continue
                live = sub > ks
                col = jnp.where(live, col, 0.0)
                base = jnp.where(here & live, 0.0, tiles[j])
            else:
                base = jnp.where(here, 0.0, tiles[j])
            tiles[j] = base - col * scaled


def ortho_kernel(gram_ref, cur_ref, list_ref, count_ref, basis_ref, p0, p1, p2, p3, inv):
    invert_rows(gram_ref[...], inv)
    full = inv[...]
    high = full.astype(BF16)
    low = (full - high.astype(F32)).astype(BF16)
    both = jnp.concatenate([high, low], axis=0)
    width = full.shape[0]

    def rotate(t, carry):
        prod = lax.dot_general(
            cur_ref[t], both, (((1,), (1,)), ((), ())), preferred_element_type=F32
        )
        basis_ref[t] = (prod[:, :width] + prod[:, width:]).astype(BF16)
        return carry

    lax.fori_loop(0, basis_ref.shape[0], rotate, 0, unroll=4)
    for d, out in enumerate((p0, p1, p2, p3)):
        for s in range(out.shape[0]):
            live = s < count_ref[0, d]

            @pl.when(live)
            def _():
                out[s] = basis_ref[list_ref[0, d, s]]

            @pl.when(jnp.logical_not(live))
            def _():
                out[s] = jnp.zeros(out.shape[1:], BF16)


def orthonormalize(gram, current, send_list, send_count):
    capacity = send_list.shape[2]
    tile = current.shape[1:]
    pack = jax.ShapeDtypeStruct((capacity,) + tile, BF16)
    return pl.pallas_call(
        ortho_kernel,
        out_shape=(jax.ShapeDtypeStruct(current.shape, BF16), pack, pack, pack, pack),
        in_specs=[VM, VM, SM, SM],
        out_specs=(VM,) * 5,
        scratch_shapes=[pltpu.VMEM(gram.shape, F32)],
        compiler_params=pltpu.CompilerParams(vmem_limit_bytes=LIMIT),
        name="ortho",
    )(gram, current, send_list, send_count)


def graph_kernel(
    scale_gram, scale_ray, row_ref, col_ref, tiles_ref, basis_ref, r0, r1, r2, r3,
    cur_ref, gram_ref, ray_ref, ext, acc,
):
    step = pl.program_id(0)
    group = tiles_ref.shape[0]
    row_tiles = basis_ref.shape[0]
    capacity = r0.shape[0]

    @pl.when(step == 0)
    def _():
        ext[0:row_tiles] = basis_ref[...]
        for d, r in enumerate((r0, r1, r2, r3)):
            first = row_tiles + d * capacity
            ext[first : first + capacity] = r[...]
        acc[...] = jnp.zeros_like(acc)

    for t in range(group):
        row = row_ref[step * group + t]
        col = col_ref[step * group + t]
        acc[row] += jnp.dot(tiles_ref[t], ext[col], preferred_element_type=F32)

    @pl.when(step == pl.num_programs(0) - 1)
    def _():
        width = gram_ref.shape[0]

        def fold(t, total):
            applied = acc[t]
            high = applied.astype(BF16)
            low = (applied - high.astype(F32)).astype(BF16)
            cur_ref[t] = high
            left = jnp.concatenate([basis_ref[t], high], axis=1)
            right = jnp.concatenate([high, low], axis=1)
            return total + lax.dot_general(
                left, right, (((0,), (0,)), ((), ())), preferred_element_type=F32
            )

        total = lax.fori_loop(
            0, row_tiles, fold, jnp.zeros((2 * width, 2 * width), F32), unroll=2
        )
        ray_ref[...] = (total[:width, :width] + total[:width, width:]) * scale_ray
        gram_ref[...] = total[width:, :width] * scale_gram


def graph(basis, received, tiles, tile_row, tile_col, node_total):
    row_tiles = basis.shape[0]
    tile = basis.shape[1:]
    stored = tiles.shape[0]
    group = next(g for g in (36, 32, 24, 16, 8, 4, 2, 1) if stored % g == 0)
    capacity = received[0].shape[0]

    def fixed(shape):
        return pl.BlockSpec(shape, lambda i: (0,) * len(shape))

    width = tile[1]
    return pl.pallas_call(
        functools.partial(graph_kernel, 1.0 / node_total, 1.0 / math.sqrt(node_total)),
        grid=(stored // group,),
        out_shape=(
            jax.ShapeDtypeStruct(basis.shape, BF16),
            jax.ShapeDtypeStruct((width, width), F32),
            jax.ShapeDtypeStruct((width, width), F32),
        ),
        in_specs=[SM, SM, pl.BlockSpec((group,) + tiles.shape[1:], lambda i: (i, 0, 0)), fixed(basis.shape)]
        + [fixed(received[0].shape)] * 4,
        out_specs=(fixed(basis.shape), fixed((width, width)), fixed((width, width))),
        scratch_shapes=[
            pltpu.VMEM((row_tiles + 4 * capacity,) + tile, BF16),
            pltpu.VMEM((row_tiles,) + tile, F32),
        ],
        compiler_params=pltpu.CompilerParams(vmem_limit_bytes=LIMIT),
        name="graph",
    )(tile_row, tile_col, tiles, basis, *received)


def exchange(packed):
    received = []
    for axis, down, up in (("dom", packed[0], packed[1]), ("region", packed[2], packed[3])):
        count = lax.axis_size(axis)
        forward = [(i, i + 1) for i in range(count - 1)]
        backward = [(i + 1, i) for i in range(count - 1)]
        received.append(lax.ppermute(down, axis, forward))
        received.append(lax.ppermute(up, axis, backward))
    return received


def shards(x_init, tiles, tile_row, tile_col, send_list, send_count):
    row_count, vectors = x_init.shape
    tile_size = tiles.shape[1]
    row_tiles = row_count // tile_size
    regions, doms = lax.axis_size("region"), lax.axis_size("dom")
    node_total = row_count * regions * doms
    part = lax.dot_general(
        x_init, x_init, (((0,), (0,)), ((), ())), preferred_element_type=F32
    ) * (1.0 / node_total)
    current = x_init.reshape(row_tiles, tile_size, vectors)
    rays = []
    for iteration in range(ITERS):
        gram = all_sum(part, regions, doms, iteration)
        basis, *packed = orthonormalize(gram, current, send_list, send_count)
        received = exchange(packed)
        current, part, ray = graph(basis, received, tiles, tile_row, tile_col, node_total)
        rays.append(ray)
    ritz = all_sum(jnp.concatenate(rays, axis=0), regions, doms, ITERS)
    return basis.reshape(row_count, vectors), ritz.reshape(ITERS, vectors, vectors)


def solution(mesh):
    both = ("region", "dom")
    in_specs = (
        P(both, None),
        P(both, None, None),
        P(both),
        P(both),
        P(both, None, None),
        P(both, None),
    )
    return jax.shard_map(
        shards, mesh=mesh, in_specs=in_specs, out_specs=(P(both, None), P()), check_vma=False
    )
```

```python
import functools
import math

import jax
import jax.numpy as jnp
from jax import lax
from jax.experimental import pallas as pl
from jax.experimental.pallas import tpu as pltpu
from jax.sharding import PartitionSpec as P

ITERS = 2
F32 = jnp.float32
BF16 = jnp.bfloat16
MESH = pl.DeviceIdType.MESH
VM = pl.BlockSpec(memory_space=pltpu.VMEM)
SM = pl.BlockSpec(memory_space=pltpu.SMEM)
LIMIT = 48 * 1024 * 1024


def reduce_kernel(regions, doms, pieces, x_ref, o_ref, scat, res, send_a, recv_a, send_b, recv_b):
    total = regions * doms
    stride = total // pieces
    me = lax.axis_index("dom") * regions + lax.axis_index("region")
    mine = me // stride
    owner = lax.rem(me, stride) == 0

    def away(off):
        flat = me + off
        flat = jnp.where(flat >= total, flat - total, flat)
        return (lax.rem(flat, regions), flat // regions)

    barrier = pltpu.get_barrier_semaphore()

    def greet(off, carry):
        pl.semaphore_signal(
            barrier, inc=1, device_id=away(off), device_id_type=MESH
        )
        return carry

    lax.fori_loop(1, total, greet, 0)
    pl.semaphore_wait(barrier, total - 1)

    def scatter(step, carry):
        piece = lax.rem(mine + step, pieces)
        target = piece * stride

        @pl.when(target != me)
        def _():
            pltpu.make_async_remote_copy(
                src_ref=x_ref.at[piece],
                dst_ref=scat.at[lax.rem(me - target - 1 + total, total)],
                send_sem=send_a,
                recv_sem=recv_a,
                device_id=(lax.rem(target, regions), target // regions),
                device_id_type=MESH,
            ).start()

        return carry

    lax.fori_loop(0, pieces, scatter, 0)

    @pl.when(owner)
    def _():
        pltpu.make_async_copy(scat, scat, recv_a).wait()
        parts = [scat[s] for s in range(total - 1)] + [x_ref[mine]]
        while len(parts) > 1:
            parts = [a + b for a, b in zip(parts[::2], parts[1::2])] + (
                [parts[-1]] if len(parts) % 2 else []
            )
        res[mine] = parts[0]

        def spread(off, carry):
            pltpu.make_async_remote_copy(
                src_ref=res.at[mine],
                dst_ref=res.at[mine],
                send_sem=send_b,
                recv_sem=recv_b,
                device_id=away(off),
                device_id_type=MESH,
            ).start()
            return carry

        lax.fori_loop(1, total, spread, 0)
        rest = res.at[pl.ds(0, pieces - 1)]
        pltpu.make_async_copy(rest, rest, recv_b).wait()
        sent = x_ref.at[pl.ds(0, pieces - 1)]
        pltpu.make_async_copy(sent, sent, send_a).wait()
        pltpu.make_async_copy(scat, scat, send_b).wait()

    @pl.when(jnp.logical_not(owner))
    def _():
        pltpu.make_async_copy(res, res, recv_b).wait()
        pltpu.make_async_copy(x_ref, x_ref, send_a).wait()

    o_ref[...] = res[...]


def all_sum(x, regions, doms, ident):
    rows, lanes = x.shape
    total = regions * doms
    pieces = min(total, 16)
    shape = (pieces, rows // pieces, lanes)
    out = pl.pallas_call(
        functools.partial(reduce_kernel, regions, doms, pieces),
        out_shape=jax.ShapeDtypeStruct(shape, F32),
        in_specs=[VM],
        out_specs=VM,
        scratch_shapes=[
            pltpu.VMEM((total - 1,) + shape[1:], F32),
            pltpu.VMEM(shape, F32),
            pltpu.SemaphoreType.DMA,
            pltpu.SemaphoreType.DMA,
            pltpu.SemaphoreType.DMA,
            pltpu.SemaphoreType.DMA,
        ],
        compiler_params=pltpu.CompilerParams(collective_id=ident, has_side_effects=True),
        name="allsum" + str(ident),
    )(x.reshape(shape))
    return out.reshape(rows, lanes)


def invert_rows(gram, out_ref):
    size = gram.shape[0]
    count = size // 8
    tiles = [gram[8 * j : 8 * j + 8, :] for j in range(count)]
    lane = lax.broadcasted_iota(jnp.int32, (8, size), 1)
    sub = lax.broadcasted_iota(jnp.int32, (8, size), 0)

    def row(tile, c):
        return jnp.broadcast_to(tile[c : c + 1, :], (8, size))

    def column(tile, c):
        return jnp.broadcast_to(tile[:, c : c + 1], (8, size))

    for kb in range(count):
        first = 8 * kb
        inside = (lane >= first) & (lane < first + 8)
        cols = [column(tiles[kb], first + c) for c in range(8)]
        rows = jnp.where(inside, jnp.where(lane == sub + first, 1.0, 0.0), tiles[kb])
        roots = jnp.zeros((8, size), F32)
        lower, scaled = [], []
        for c in range(8):
            pivot = row(cols[c], c)
            root = lax.rsqrt(pivot)
            root = root * (1.5 - 0.5 * pivot * root * root)
            roots = jnp.where(sub == c, root, roots)
            ratio = cols[c] * (root * root)
            mine = row(rows, c)
            scaled.append(mine * (root * root))
            lower.append(ratio)
            if c < 7:
                rows = rows - jnp.where(sub > c, ratio, 0.0) * mine
                for later in range(c + 1, 8):
                    cols[later] = cols[later] - ratio * row(cols[c], later)
        out_ref[first : first + 8, :] = jnp.where(lane <= sub + first, rows * roots, 0.0)
        for i in range(7, 0, -1):
            for c in range(i):
                scaled[c] = scaled[c] - row(lower[c], i) * scaled[i]
        for j in range(kb + 1, count):
            terms = [column(tiles[j], first + c) * scaled[c] for c in range(8)]
            while len(terms) > 1:
                terms = [p + q for p, q in zip(terms[::2], terms[1::2])]
            tiles[j] = jnp.where(inside, 0.0, tiles[j]) - terms[0]


def invert_kernel(gram_ref, both_ref, inv):
    width = gram_ref.shape[0]
    invert_rows(gram_ref[...], inv)
    full = inv[...]
    high = full.astype(BF16)
    both_ref[0:width] = high
    both_ref[width : 2 * width] = (full - high.astype(F32)).astype(BF16)


def inverse_factor(gram):
    width = gram.shape[0]
    return pl.pallas_call(
        invert_kernel,
        out_shape=jax.ShapeDtypeStruct((2 * width, width), BF16),
        in_specs=[VM],
        out_specs=VM,
        scratch_shapes=[pltpu.VMEM(gram.shape, F32)],
        name="invert",
    )(gram)


def halo_kernel(regions, doms, both_ref, cur_ref, list_ref, ext_ref, own, send, send_sem, recv_sem):
    region, dom = lax.axis_index("region"), lax.axis_index("dom")
    capacity = send.shape[1]
    row_tiles = cur_ref.shape[0]
    width = cur_ref.shape[2]
    ways = (
        ((region, dom + 1), dom < doms - 1, dom > 0),
        ((region, dom - 1), dom > 0, dom < doms - 1),
        ((region + 1, dom), region < regions - 1, region > 0),
        ((region - 1, dom), region > 0, region < regions - 1),
    )
    barrier = pltpu.get_barrier_semaphore()
    for target, there, _ in ways:

        @pl.when(there)
        def _():
            pl.semaphore_signal(barrier, inc=1, device_id=target, device_id_type=MESH)

    both = both_ref[...]

    def rotate(t, carry):
        prod = lax.dot_general(
            cur_ref[t], both, (((1,), (1,)), ((), ())), preferred_element_type=F32
        )
        basis = (prod[:, :width] + prod[:, width:]).astype(BF16)
        ext_ref[t] = basis
        own[t] = basis
        return carry

    lax.fori_loop(0, row_tiles, rotate, 0, unroll=4)
    pl.semaphore_wait(barrier, sum(there.astype(jnp.int32) for _, there, _ in ways))

    def copy(d):
        return pltpu.make_async_remote_copy(
            src_ref=send.at[d],
            dst_ref=ext_ref.at[pl.ds(row_tiles + d * capacity, capacity)],
            send_sem=send_sem.at[d],
            recv_sem=recv_sem.at[d],
            device_id=ways[d][0],
            device_id_type=MESH,
        )

    for d in range(4):

        def pick(s, carry):
            send[d, s] = own[list_ref[0, d, s]]
            return carry

        lax.fori_loop(0, capacity, pick, 0, unroll=True)

    for d in range(4):

        @pl.when(ways[d][1])
        def _():
            copy(d).start()

    for d in range(4):

        @pl.when(ways[d][1])
        def _():
            copy(d).wait_send()

        @pl.when(ways[d][2])
        def _():
            copy(d).wait_recv()


def exchange(both, current, send_list, regions, doms, ident):
    capacity = send_list.shape[2]
    row_tiles = current.shape[0]
    tile = current.shape[1:]
    return pl.pallas_call(
        functools.partial(halo_kernel, regions, doms),
        out_shape=jax.ShapeDtypeStruct((row_tiles + 4 * capacity,) + tile, BF16),
        in_specs=[VM, VM, SM],
        out_specs=VM,
        scratch_shapes=[
            pltpu.VMEM(current.shape, BF16),
            pltpu.VMEM((4, capacity) + tile, BF16),
            pltpu.SemaphoreType.DMA((4,)),
            pltpu.SemaphoreType.DMA((4,)),
        ],
        compiler_params=pltpu.CompilerParams(
            collective_id=ident, has_side_effects=True, vmem_limit_bytes=LIMIT
        ),
        name="halo" + str(ident),
    )(both, current, send_list)


def graph_kernel(
    scale_gram, scale_ray, last, row_ref, col_ref, tiles_ref, ext, cur_ref, gram_ref, ray_ref, acc,
):
    step = pl.program_id(0)
    group = tiles_ref.shape[0]
    row_tiles = acc.shape[0]

    @pl.when(step == 0)
    def _():
        acc[...] = jnp.zeros_like(acc)

    for t in range(group):
        row = row_ref[step * group + t]
        col = col_ref[step * group + t]
        acc[row] += jnp.dot(tiles_ref[t], ext[col], preferred_element_type=F32)

    @pl.when(step == pl.num_programs(0) - 1)
    def _():
        width = gram_ref.shape[0]

        def fold(t, total):
            applied = acc[t]
            high = applied.astype(BF16)
            low = (applied - high.astype(F32)).astype(BF16)
            cur_ref[t] = ext[t] if last else high
            left = jnp.concatenate([ext[t], high], axis=1)
            right = jnp.concatenate([high, low], axis=1)
            return total + lax.dot_general(
                left, right, (((0,), (0,)), ((), ())), preferred_element_type=F32
            )

        total = lax.fori_loop(
            0, row_tiles, fold, jnp.zeros((2 * width, 2 * width), F32), unroll=2
        )
        ray_ref[...] = (total[:width, :width] + total[:width, width:]) * scale_ray
        gram_ref[...] = total[width:, :width] * scale_gram


def graph(ext, tiles, tile_row, tile_col, row_tiles, node_total, last):
    tile = ext.shape[1:]
    stored = tiles.shape[0]
    group = next(g for g in (36, 32, 24, 16, 8, 4, 2, 1) if stored % g == 0)
    width = tile[1]

    def fixed(shape):
        return pl.BlockSpec(shape, lambda i: (0,) * len(shape))

    own = (row_tiles,) + tile
    return pl.pallas_call(
        functools.partial(graph_kernel, 1.0 / node_total, 1.0 / math.sqrt(node_total), last),
        grid=(stored // group,),
        out_shape=(
            jax.ShapeDtypeStruct(own, BF16),
            jax.ShapeDtypeStruct((width, width), F32),
            jax.ShapeDtypeStruct((width, width), F32),
        ),
        in_specs=[
            SM,
            SM,
            pl.BlockSpec((group,) + tiles.shape[1:], lambda i: (i, 0, 0)),
            fixed(ext.shape),
        ],
        out_specs=(fixed(own), fixed((width, width)), fixed((width, width))),
        scratch_shapes=[pltpu.VMEM(own, F32)],
        compiler_params=pltpu.CompilerParams(vmem_limit_bytes=LIMIT),
        name="graph",
    )(tile_row, tile_col, tiles, ext)


def shards(x_init, tiles, tile_row, tile_col, send_list, send_count):
    row_count, vectors = x_init.shape
    tile_size = tiles.shape[1]
    row_tiles = row_count // tile_size
    regions, doms = lax.axis_size("region"), lax.axis_size("dom")
    node_total = row_count * regions * doms
    part = lax.dot_general(
        x_init, x_init, (((0,), (0,)), ((), ())), preferred_element_type=F32
    ) * (1.0 / node_total)
    current = x_init.reshape(row_tiles, tile_size, vectors)
    rays = []
    for iteration in range(ITERS):
        gram = all_sum(part, regions, doms, iteration)
        both = inverse_factor(gram)
        ext = exchange(both, current, send_list, regions, doms, ITERS + 1 + iteration)
        current, part, ray = graph(
            ext, tiles, tile_row, tile_col, row_tiles, node_total, iteration == ITERS - 1
        )
        rays.append(ray)
    ritz = all_sum(jnp.concatenate(rays, axis=0), regions, doms, ITERS)
    return current.reshape(row_count, vectors), ritz.reshape(ITERS, vectors, vectors)


def solution(mesh):
    both = ("region", "dom")
    in_specs = (
        P(both, None),
        P(both, None, None),
        P(both),
        P(both),
        P(both, None, None),
        P(both, None),
    )
    return jax.shard_map(
        shards, mesh=mesh, in_specs=in_specs, out_specs=(P(both, None), P()), check_vma=False
    )
```

```python
import functools
import math

import jax
import jax.numpy as jnp
from jax import lax
from jax.experimental import pallas as pl
from jax.experimental.pallas import tpu as pltpu
from jax.sharding import PartitionSpec as P

ITERS = 2
F32 = jnp.float32
BF16 = jnp.bfloat16
MESH = pl.DeviceIdType.MESH
VM = pl.BlockSpec(memory_space=pltpu.VMEM)
SM = pl.BlockSpec(memory_space=pltpu.SMEM)
LIMIT = 48 * 1024 * 1024


def reduce_kernel(regions, doms, x_ref, o_ref, part, column, res, send_a, recv_a, send_b, recv_b, send_c, recv_c):
    region, dom = lax.axis_index("region"), lax.axis_index("dom")

    def across(off):
        target = region + off
        return jnp.where(target >= regions, target - regions, target)

    def along(off):
        target = dom + off
        return jnp.where(target >= doms, target - doms, target)

    barrier = pltpu.get_barrier_semaphore()
    for off in range(1, regions):
        pl.semaphore_signal(barrier, inc=1, device_id=(across(off), dom), device_id_type=MESH)
    for off in range(1, doms):
        pl.semaphore_signal(barrier, inc=1, device_id=(region, along(off)), device_id_type=MESH)
    part[region] = x_ref[region]
    pl.semaphore_wait(barrier, regions + doms - 2)

    def send(src, dst, sems, off, target):
        copy = pltpu.make_async_remote_copy(
            src_ref=src,
            dst_ref=dst,
            send_sem=sems[0].at[off - 1],
            recv_sem=sems[1].at[off - 1],
            device_id=target,
            device_id_type=MESH,
        )
        copy.start()
        return copy

    first = [
        send(x_ref.at[across(o)], part.at[region], (send_a, recv_a), o, (across(o), dom))
        for o in range(1, regions)
    ]
    for copy in first:
        copy.wait_recv()
    column[dom] = jnp.sum(part[...], axis=0)
    second = [
        send(column.at[dom], column.at[dom], (send_b, recv_b), o, (region, along(o)))
        for o in range(1, doms)
    ]
    for copy in second:
        copy.wait_recv()
    res[region] = jnp.sum(column[...], axis=0)
    third = [
        send(res.at[region], res.at[region], (send_c, recv_c), o, (across(o), dom))
        for o in range(1, regions)
    ]
    for copy in third:
        copy.wait_recv()
    o_ref[...] = res[...]
    for copy in first + second + third:
        copy.wait_send()


def all_sum(x, regions, doms, ident):
    rows, lanes = x.shape
    piece = (rows // regions, lanes)
    shape = (regions,) + piece
    out = pl.pallas_call(
        functools.partial(reduce_kernel, regions, doms),
        out_shape=jax.ShapeDtypeStruct(shape, F32),
        in_specs=[VM],
        out_specs=VM,
        scratch_shapes=[
            pltpu.VMEM(shape, F32),
            pltpu.VMEM((doms,) + piece, F32),
            pltpu.VMEM(shape, F32),
        ]
        + [
            pltpu.SemaphoreType.DMA((count - 1,))
            for count in (regions, regions, doms, doms, regions, regions)
        ],
        compiler_params=pltpu.CompilerParams(collective_id=ident, has_side_effects=True),
        name="allsum" + str(ident),
    )(x.reshape(shape))
    return out.reshape(rows, lanes)


def invert_rows(gram, out_ref):
    size = gram.shape[0]
    count = size // 8
    tiles = [gram[8 * j : 8 * j + 8, :] for j in range(count)]
    lane = lax.broadcasted_iota(jnp.int32, (8, size), 1)
    sub = lax.broadcasted_iota(jnp.int32, (8, size), 0)

    def row(tile, c):
        return jnp.broadcast_to(tile[c : c + 1, :], (8, size))

    def column(tile, c):
        return jnp.broadcast_to(tile[:, c : c + 1], (8, size))

    for kb in range(count):
        first = 8 * kb
        inside = (lane >= first) & (lane < first + 8)
        cols = [column(tiles[kb], first + c) for c in range(8)]
        rows = jnp.where(inside, jnp.where(lane == sub + first, 1.0, 0.0), tiles[kb])
        roots = jnp.zeros((8, size), F32)
        lower, scaled = [], []
        for c in range(8):
            pivot = row(cols[c], c)
            root = lax.rsqrt(pivot)
            root = root * (1.5 - 0.5 * pivot * root * root)
            roots = jnp.where(sub == c, root, roots)
            ratio = cols[c] * (root * root)
            mine = row(rows, c)
            scaled.append(mine * (root * root))
            lower.append(ratio)
            if c < 7:
                rows = rows - jnp.where(sub > c, ratio, 0.0) * mine
                for later in range(c + 1, 8):
                    cols[later] = cols[later] - ratio * row(cols[c], later)
        out_ref[first : first + 8, :] = jnp.where(lane <= sub + first, rows * roots, 0.0)
        for i in range(7, 0, -1):
            for c in range(i):
                scaled[c] = scaled[c] - row(lower[c], i) * scaled[i]
        for j in range(kb + 1, count):
            terms = [column(tiles[j], first + c) * scaled[c] for c in range(8)]
            while len(terms) > 1:
                terms = [p + q for p, q in zip(terms[::2], terms[1::2])]
            tiles[j] = jnp.where(inside, 0.0, tiles[j]) - terms[0]


def invert_kernel(gram_ref, both_ref, inv):
    width = gram_ref.shape[0]
    invert_rows(gram_ref[...], inv)
    full = inv[...]
    high = full.astype(BF16)
    both_ref[0:width] = high
    both_ref[width : 2 * width] = (full - high.astype(F32)).astype(BF16)


def inverse_factor(gram):
    width = gram.shape[0]
    return pl.pallas_call(
        invert_kernel,
        out_shape=jax.ShapeDtypeStruct((2 * width, width), BF16),
        in_specs=[VM],
        out_specs=VM,
        scratch_shapes=[pltpu.VMEM(gram.shape, F32)],
        name="invert",
    )(gram)


def halo_kernel(regions, doms, both_ref, cur_ref, list_ref, ext_ref, own, send, send_sem, recv_sem):
    region, dom = lax.axis_index("region"), lax.axis_index("dom")
    capacity = send.shape[1]
    row_tiles = cur_ref.shape[0]
    width = cur_ref.shape[2]
    ways = (
        ((region, dom + 1), dom < doms - 1, dom > 0),
        ((region, dom - 1), dom > 0, dom < doms - 1),
        ((region + 1, dom), region < regions - 1, region > 0),
        ((region - 1, dom), region > 0, region < regions - 1),
    )
    barrier = pltpu.get_barrier_semaphore()
    for target, there, _ in ways:

        @pl.when(there)
        def _():
            pl.semaphore_signal(barrier, inc=1, device_id=target, device_id_type=MESH)

    both = both_ref[...]

    def rotate(t, carry):
        prod = lax.dot_general(
            cur_ref[t], both, (((1,), (1,)), ((), ())), preferred_element_type=F32
        )
        basis = (prod[:, :width] + prod[:, width:]).astype(BF16)
        ext_ref[t] = basis
        own[t] = basis
        return carry

    lax.fori_loop(0, row_tiles, rotate, 0, unroll=4)
    pl.semaphore_wait(barrier, sum(there.astype(jnp.int32) for _, there, _ in ways))

    def copy(d):
        return pltpu.make_async_remote_copy(
            src_ref=send.at[d],
            dst_ref=ext_ref.at[pl.ds(row_tiles + d * capacity, capacity)],
            send_sem=send_sem.at[d],
            recv_sem=recv_sem.at[d],
            device_id=ways[d][0],
            device_id_type=MESH,
        )

    for d in range(4):

        def pick(s, carry):
            send[d, s] = own[list_ref[0, d, s]]
            return carry

        lax.fori_loop(0, capacity, pick, 0, unroll=True)

    for d in range(4):

        @pl.when(ways[d][1])
        def _():
            copy(d).start()

    for d in range(4):

        @pl.when(ways[d][1])
        def _():
            copy(d).wait_send()

        @pl.when(ways[d][2])
        def _():
            copy(d).wait_recv()


def exchange(both, current, send_list, regions, doms, ident):
    capacity = send_list.shape[2]
    row_tiles = current.shape[0]
    tile = current.shape[1:]
    return pl.pallas_call(
        functools.partial(halo_kernel, regions, doms),
        out_shape=jax.ShapeDtypeStruct((row_tiles + 4 * capacity,) + tile, BF16),
        in_specs=[VM, VM, SM],
        out_specs=VM,
        scratch_shapes=[
            pltpu.VMEM(current.shape, BF16),
            pltpu.VMEM((4, capacity) + tile, BF16),
            pltpu.SemaphoreType.DMA((4,)),
            pltpu.SemaphoreType.DMA((4,)),
        ],
        compiler_params=pltpu.CompilerParams(
            collective_id=ident, has_side_effects=True, vmem_limit_bytes=LIMIT
        ),
        name="halo" + str(ident),
    )(both, current, send_list)


def graph_kernel(
    scale_gram, scale_ray, last, row_ref, col_ref, tiles_ref, ext, cur_ref, gram_ref, ray_ref, acc,
):
    step = pl.program_id(0)
    group = tiles_ref.shape[0]
    row_tiles = acc.shape[0]

    @pl.when(step == 0)
    def _():
        acc[...] = jnp.zeros_like(acc)

    for t in range(group):
        row = row_ref[step * group + t]
        col = col_ref[step * group + t]
        acc[row] += jnp.dot(tiles_ref[t], ext[col], preferred_element_type=F32)

    @pl.when(step == pl.num_programs(0) - 1)
    def _():
        width = gram_ref.shape[0]

        def fold(t, total):
            applied = acc[t]
            high = applied.astype(BF16)
            low = (applied - high.astype(F32)).astype(BF16)
            cur_ref[t] = ext[t] if last else high
            left = jnp.concatenate([ext[t], high], axis=1)
            right = jnp.concatenate([high, low], axis=1)
            return total + lax.dot_general(
                left, right, (((0,), (0,)), ((), ())), preferred_element_type=F32
            )

        total = lax.fori_loop(
            0, row_tiles, fold, jnp.zeros((2 * width, 2 * width), F32), unroll=2
        )
        ray_ref[...] = (total[:width, :width] + total[:width, width:]) * scale_ray
        gram_ref[...] = total[width:, :width] * scale_gram


def graph(ext, tiles, tile_row, tile_col, row_tiles, node_total, last):
    tile = ext.shape[1:]
    stored = tiles.shape[0]
    group = next(g for g in (36, 32, 24, 16, 8, 4, 2, 1) if stored % g == 0)
    width = tile[1]

    def fixed(shape):
        return pl.BlockSpec(shape, lambda i: (0,) * len(shape))

    own = (row_tiles,) + tile
    return pl.pallas_call(
        functools.partial(graph_kernel, 1.0 / node_total, 1.0 / math.sqrt(node_total), last),
        grid=(stored // group,),
        out_shape=(
            jax.ShapeDtypeStruct(own, BF16),
            jax.ShapeDtypeStruct((width, width), F32),
            jax.ShapeDtypeStruct((width, width), F32),
        ),
        in_specs=[
            SM,
            SM,
            pl.BlockSpec((group,) + tiles.shape[1:], lambda i: (i, 0, 0)),
            fixed(ext.shape),
        ],
        out_specs=(fixed(own), fixed((width, width)), fixed((width, width))),
        scratch_shapes=[pltpu.VMEM(own, F32)],
        compiler_params=pltpu.CompilerParams(vmem_limit_bytes=LIMIT),
        name="graph",
    )(tile_row, tile_col, tiles, ext)


def shards(x_init, tiles, tile_row, tile_col, send_list, send_count):
    row_count, vectors = x_init.shape
    tile_size = tiles.shape[1]
    row_tiles = row_count // tile_size
    regions, doms = lax.axis_size("region"), lax.axis_size("dom")
    node_total = row_count * regions * doms
    part = lax.dot_general(
        x_init, x_init, (((0,), (0,)), ((), ())), preferred_element_type=F32
    ) * (1.0 / node_total)
    current = x_init.reshape(row_tiles, tile_size, vectors)
    rays = []
    for iteration in range(ITERS):
        gram = all_sum(part, regions, doms, iteration)
        both = inverse_factor(gram)
        ext = exchange(both, current, send_list, regions, doms, ITERS + 1 + iteration)
        current, part, ray = graph(
            ext, tiles, tile_row, tile_col, row_tiles, node_total, iteration == ITERS - 1
        )
        rays.append(ray)
    ritz = all_sum(jnp.concatenate(rays, axis=0), regions, doms, ITERS)
    return current.reshape(row_count, vectors), ritz.reshape(ITERS, vectors, vectors)


def solution(mesh):
    both = ("region", "dom")
    in_specs = (
        P(both, None),
        P(both, None, None),
        P(both),
        P(both),
        P(both, None, None),
        P(both, None),
    )
    return jax.shard_map(
        shards, mesh=mesh, in_specs=in_specs, out_specs=(P(both, None), P()), check_vma=False
    )
```

```python
import functools
import math

import jax
import jax.numpy as jnp
from jax import lax
from jax.experimental import pallas as pl
from jax.experimental.pallas import tpu as pltpu
from jax.sharding import PartitionSpec as P

ITERS = 2
F32 = jnp.float32
BF16 = jnp.bfloat16
MESH = pl.DeviceIdType.MESH
VM = pl.BlockSpec(memory_space=pltpu.VMEM)
SM = pl.BlockSpec(memory_space=pltpu.SMEM)
LIMIT = 48 * 1024 * 1024


def reduce_kernel(regions, doms, pieces, x_ref, o_ref, scat, res, send_a, recv_a, send_b, recv_b):
    total = regions * doms
    stride = total // pieces
    me = lax.axis_index("dom") * regions + lax.axis_index("region")
    mine = me // stride
    owner = lax.rem(me, stride) == 0

    def away(off):
        flat = me + off
        flat = jnp.where(flat >= total, flat - total, flat)
        return (lax.rem(flat, regions), flat // regions)

    barrier = pltpu.get_barrier_semaphore()

    def greet(off, carry):
        pl.semaphore_signal(
            barrier, inc=1, device_id=away(off), device_id_type=MESH
        )
        return carry

    lax.fori_loop(1, total, greet, 0)
    pl.semaphore_wait(barrier, total - 1)

    def scatter(step, carry):
        piece = lax.rem(mine + step, pieces)
        target = piece * stride

        @pl.when(target != me)
        def _():
            pltpu.make_async_remote_copy(
                src_ref=x_ref.at[piece],
                dst_ref=scat.at[lax.rem(me - target - 1 + total, total)],
                send_sem=send_a,
                recv_sem=recv_a,
                device_id=(lax.rem(target, regions), target // regions),
                device_id_type=MESH,
            ).start()

        return carry

    lax.fori_loop(0, pieces, scatter, 0)

    @pl.when(owner)
    def _():
        pltpu.make_async_copy(scat, scat, recv_a).wait()
        parts = [scat[s] for s in range(total - 1)] + [x_ref[mine]]
        while len(parts) > 1:
            parts = [a + b for a, b in zip(parts[::2], parts[1::2])] + (
                [parts[-1]] if len(parts) % 2 else []
            )
        res[mine] = parts[0]

        def spread(off, carry):
            pltpu.make_async_remote_copy(
                src_ref=res.at[mine],
                dst_ref=res.at[mine],
                send_sem=send_b,
                recv_sem=recv_b,
                device_id=away(off),
                device_id_type=MESH,
            ).start()
            return carry

        lax.fori_loop(1, total, spread, 0)
        rest = res.at[pl.ds(0, pieces - 1)]
        pltpu.make_async_copy(rest, rest, recv_b).wait()
        sent = x_ref.at[pl.ds(0, pieces - 1)]
        pltpu.make_async_copy(sent, sent, send_a).wait()
        pltpu.make_async_copy(scat, scat, send_b).wait()

    @pl.when(jnp.logical_not(owner))
    def _():
        pltpu.make_async_copy(res, res, recv_b).wait()
        pltpu.make_async_copy(x_ref, x_ref, send_a).wait()

    o_ref[...] = res[...]


def all_sum(x, regions, doms, ident):
    rows, lanes = x.shape
    total = regions * doms
    pieces = min(total, 16)
    shape = (pieces, rows // pieces, lanes)
    out = pl.pallas_call(
        functools.partial(reduce_kernel, regions, doms, pieces),
        out_shape=jax.ShapeDtypeStruct(shape, F32),
        in_specs=[VM],
        out_specs=VM,
        scratch_shapes=[
            pltpu.VMEM((total - 1,) + shape[1:], F32),
            pltpu.VMEM(shape, F32),
            pltpu.SemaphoreType.DMA,
            pltpu.SemaphoreType.DMA,
            pltpu.SemaphoreType.DMA,
            pltpu.SemaphoreType.DMA,
        ],
        compiler_params=pltpu.CompilerParams(collective_id=ident, has_side_effects=True),
        name="allsum" + str(ident),
    )(x.reshape(shape))
    return out.reshape(rows, lanes)


def invert_rows(gram, out_ref):
    size = gram.shape[0]
    count = size // 8
    tiles = [gram[8 * j : 8 * j + 8, :] for j in range(count)]
    lane = lax.broadcasted_iota(jnp.int32, (8, size), 1)
    sub = lax.broadcasted_iota(jnp.int32, (8, size), 0)

    def row(tile, c):
        return jnp.broadcast_to(tile[c : c + 1, :], (8, size))

    def column(tile, c):
        return jnp.broadcast_to(tile[:, c : c + 1], (8, size))

    for kb in range(count):
        first = 8 * kb
        inside = (lane >= first) & (lane < first + 8)
        cols = [column(tiles[kb], first + c) for c in range(8)]
        rows = jnp.where(inside, jnp.where(lane == sub + first, 1.0, 0.0), tiles[kb])
        roots = jnp.zeros((8, size), F32)
        lower, scaled = [], []
        for c in range(8):
            pivot = row(cols[c], c)
            root = lax.rsqrt(pivot)
            root = root * (1.5 - 0.5 * pivot * root * root)
            roots = jnp.where(sub == c, root, roots)
            ratio = cols[c] * (root * root)
            mine = row(rows, c)
            scaled.append(mine * (root * root))
            lower.append(ratio)
            if c < 7:
                rows = rows - jnp.where(sub > c, ratio, 0.0) * mine
                for later in range(c + 1, 8):
                    cols[later] = cols[later] - ratio * row(cols[c], later)
        out_ref[first : first + 8, :] = jnp.where(lane <= sub + first, rows * roots, 0.0)
        for i in range(7, 0, -1):
            for c in range(i):
                scaled[c] = scaled[c] - row(lower[c], i) * scaled[i]
        for j in range(kb + 1, count):
            terms = [column(tiles[j], first + c) * scaled[c] for c in range(8)]
            while len(terms) > 1:
                terms = [p + q for p, q in zip(terms[::2], terms[1::2])]
            tiles[j] = jnp.where(inside, 0.0, tiles[j]) - terms[0]


def invert_kernel(gram_ref, both_ref, inv):
    width = gram_ref.shape[0]
    invert_rows(gram_ref[...], inv)
    full = inv[...]
    high = full.astype(BF16)
    both_ref[0:width] = high
    both_ref[width : 2 * width] = (full - high.astype(F32)).astype(BF16)


def inverse_factor(gram):
    width = gram.shape[0]
    return pl.pallas_call(
        invert_kernel,
        out_shape=jax.ShapeDtypeStruct((2 * width, width), BF16),
        in_specs=[VM],
        out_specs=VM,
        scratch_shapes=[pltpu.VMEM(gram.shape, F32)],
        name="invert",
    )(gram)


def halo_kernel(regions, doms, both_ref, cur_ref, list_ref, ext_ref, own, send, send_sem, recv_sem):
    region, dom = lax.axis_index("region"), lax.axis_index("dom")
    capacity = send.shape[1]
    row_tiles = cur_ref.shape[0]
    width = cur_ref.shape[2]
    ways = (
        ((region, dom + 1), dom < doms - 1, dom > 0),
        ((region, dom - 1), dom > 0, dom < doms - 1),
        ((region + 1, dom), region < regions - 1, region > 0),
        ((region - 1, dom), region > 0, region < regions - 1),
    )
    barrier = pltpu.get_barrier_semaphore()
    for target, there, _ in ways:

        @pl.when(there)
        def _():
            pl.semaphore_signal(barrier, inc=1, device_id=target, device_id_type=MESH)

    both = both_ref[...]

    def rotate(t, carry):
        prod = lax.dot_general(
            cur_ref[t], both, (((1,), (1,)), ((), ())), preferred_element_type=F32
        )
        basis = (prod[:, :width] + prod[:, width:]).astype(BF16)
        ext_ref[t] = basis
        own[t] = basis
        return carry

    lax.fori_loop(0, row_tiles, rotate, 0, unroll=4)
    pl.semaphore_wait(barrier, sum(there.astype(jnp.int32) for _, there, _ in ways))

    def copy(d):
        return pltpu.make_async_remote_copy(
            src_ref=send.at[d],
            dst_ref=ext_ref.at[pl.ds(row_tiles + d * capacity, capacity)],
            send_sem=send_sem.at[d],
            recv_sem=recv_sem.at[d],
            device_id=ways[d][0],
            device_id_type=MESH,
        )

    for d in range(4):

        def pick(s, carry):
            send[d, s] = own[list_ref[0, d, s]]
            return carry

        lax.fori_loop(0, capacity, pick, 0, unroll=True)

    for d in range(4):

        @pl.when(ways[d][1])
        def _():
            copy(d).start()

    for d in range(4):

        @pl.when(ways[d][1])
        def _():
            copy(d).wait_send()

        @pl.when(ways[d][2])
        def _():
            copy(d).wait_recv()


def exchange(both, current, send_list, regions, doms, ident):
    capacity = send_list.shape[2]
    row_tiles = current.shape[0]
    tile = current.shape[1:]
    return pl.pallas_call(
        functools.partial(halo_kernel, regions, doms),
        out_shape=jax.ShapeDtypeStruct((row_tiles + 4 * capacity,) + tile, BF16),
        in_specs=[VM, VM, SM],
        out_specs=VM,
        scratch_shapes=[
            pltpu.VMEM(current.shape, BF16),
            pltpu.VMEM((4, capacity) + tile, BF16),
            pltpu.SemaphoreType.DMA((4,)),
            pltpu.SemaphoreType.DMA((4,)),
        ],
        compiler_params=pltpu.CompilerParams(
            collective_id=ident, has_side_effects=True, vmem_limit_bytes=LIMIT
        ),
        name="halo" + str(ident),
    )(both, current, send_list)


def graph_kernel(
    scale_gram, scale_ray, last, row_ref, col_ref, tiles_ref, ext, cur_ref, gram_ref, ray_ref, acc,
):
    step = pl.program_id(0)
    group = tiles_ref.shape[0]
    row_tiles = acc.shape[0]

    @pl.when(step == 0)
    def _():
        acc[...] = jnp.zeros_like(acc)

    for start in range(0, group, 2):
        batch = range(start, min(start + 2, group))
        products = [
            jnp.dot(tiles_ref[t], ext[col_ref[step * group + t]], preferred_element_type=F32)
            for t in batch
        ]
        for t, product in zip(batch, products):
            acc[row_ref[step * group + t]] += product

    @pl.when(step == pl.num_programs(0) - 1)
    def _():
        width = gram_ref.shape[0]

        def fold(t, total):
            applied = acc[t]
            high = applied.astype(BF16)
            low = (applied - high.astype(F32)).astype(BF16)
            cur_ref[t] = ext[t] if last else high
            left = jnp.concatenate([ext[t], high], axis=1)
            right = jnp.concatenate([high, low], axis=1)
            return total + lax.dot_general(
                left, right, (((0,), (0,)), ((), ())), preferred_element_type=F32
            )

        total = lax.fori_loop(
            0, row_tiles, fold, jnp.zeros((2 * width, 2 * width), F32), unroll=2
        )
        ray_ref[...] = (total[:width, :width] + total[:width, width:]) * scale_ray
        gram_ref[...] = total[width:, :width] * scale_gram


def graph(ext, tiles, tile_row, tile_col, row_tiles, node_total, last):
    tile = ext.shape[1:]
    stored = tiles.shape[0]
    group = next(g for g in (36, 32, 24, 16, 8, 4, 2, 1) if stored % g == 0)
    width = tile[1]

    def fixed(shape):
        return pl.BlockSpec(shape, lambda i: (0,) * len(shape))

    own = (row_tiles,) + tile
    return pl.pallas_call(
        functools.partial(graph_kernel, 1.0 / node_total, 1.0 / math.sqrt(node_total), last),
        grid=(stored // group,),
        out_shape=(
            jax.ShapeDtypeStruct(own, BF16),
            jax.ShapeDtypeStruct((width, width), F32),
            jax.ShapeDtypeStruct((width, width), F32),
        ),
        in_specs=[
            SM,
            SM,
            pl.BlockSpec((group,) + tiles.shape[1:], lambda i: (i, 0, 0)),
            fixed(ext.shape),
        ],
        out_specs=(fixed(own), fixed((width, width)), fixed((width, width))),
        scratch_shapes=[pltpu.VMEM(own, F32)],
        compiler_params=pltpu.CompilerParams(vmem_limit_bytes=LIMIT),
        name="graph",
    )(tile_row, tile_col, tiles, ext)


def shards(x_init, tiles, tile_row, tile_col, send_list, send_count):
    row_count, vectors = x_init.shape
    tile_size = tiles.shape[1]
    row_tiles = row_count // tile_size
    regions, doms = lax.axis_size("region"), lax.axis_size("dom")
    node_total = row_count * regions * doms
    part = lax.dot_general(
        x_init, x_init, (((0,), (0,)), ((), ())), preferred_element_type=F32
    ) * (1.0 / node_total)
    current = x_init.reshape(row_tiles, tile_size, vectors)
    rays = []
    for iteration in range(ITERS):
        gram = all_sum(part, regions, doms, iteration)
        both = inverse_factor(gram)
        ext = exchange(both, current, send_list, regions, doms, ITERS + 1 + iteration)
        current, part, ray = graph(
            ext, tiles, tile_row, tile_col, row_tiles, node_total, iteration == ITERS - 1
        )
        rays.append(ray)
    ritz = all_sum(jnp.concatenate(rays, axis=0), regions, doms, ITERS)
    return current.reshape(row_count, vectors), ritz.reshape(ITERS, vectors, vectors)


def solution(mesh):
    both = ("region", "dom")
    in_specs = (
        P(both, None),
        P(both, None, None),
        P(both),
        P(both),
        P(both, None, None),
        P(both, None),
    )
    return jax.shard_map(
        shards, mesh=mesh, in_specs=in_specs, out_specs=(P(both, None), P()), check_vma=False
    )
```
